32 devices in a mesh: groups: 2 (over y), cell: 8 (over z, x), dp: 2 (over core).
Axes of the slice: x: 2, y: 2, z: 4, core: 2. Of those that a mesh axis runs over, the one named last changes fastest.
Arguments:
- sensitivity: bfloat16 [8192, 8192], P(('groups', 'dp'), 'cell'), parts along dimension 0, may hold values from -127 to 127
- block_scale: float32 [64, 64], P(('groups', 'dp'), 'cell'), parts along dimension 0, may hold values from 1.5134991e-05 to 0.00136214919
- depth_weight: float32 [16384], P(('groups', 'cell')), parts along dimension 0, may hold values from 0.05 to 1.5
- model: float32 [128, 8192], P('groups', 'cell'), parts along dimension 0, may hold values from -6 to 6
- residual: float32 [128, 4096], P('groups', 'dp'), parts along dimension 0, may hold values from -6 to 6
- direction: float32 [128, 8192], P('groups', 'cell'), parts along dimension 0, may hold values from -3 to 3
- gamma: float32 [128], P('groups'), parts along dimension 0, may hold values from 8192 to 32768
Outputs:
- model_new: float32 [128, 8192], P('groups', 'cell'), parts along dimension 0
- residual_new: float32 [128, 4096], P('groups', 'dp'), parts along dimension 0
- direction_new: float32 [128, 8192], P('groups', 'cell'), parts along dimension 0
- gamma_new: float32 [128], P('groups'), parts along dimension 0
The draws below stay inside these ranges and needn't reach their ends.
There are 2 independent parts, one for each index of `groups`. The reference program is written for one: setup_inputs(seed, part) draws one part's arguments, and reference() takes and returns one part's arrays. A program takes and returns all parts, laid end to end along the dimension named above; each array names one. Nothing has to cross between parts.
All inputs are finite; a program needn't handle non-finite values.
Results may differ from the reference program's by a relative error of at most 0.0025.
Values sent between devices are 32-bit elements; how exact they have to be, the bound alone decides.
A program may use at most 64 MiB of HBM per device.

```python
import math
import jax
import jax.numpy as jnp
from jax import lax

CELLS_DEV = 1024
NSETS = 64
BLOCK = 128
NDATA = 4096
NCELL = 8192


def draw_sensitivity(key, part):
    key = jax.random.fold_in(key, 1)
    values = jax.random.randint(key, (NDATA, NCELL), -127, 128, dtype=jnp.int32)
    return values.astype(jnp.float32).astype(jnp.bfloat16)


def draw_block_scale(key, part):
    key = jax.random.fold_in(key, 2)
    row_blocks = NDATA // BLOCK
    col_blocks = NCELL // BLOCK
    row_pos = jnp.arange(row_blocks, dtype=jnp.float32) / max(row_blocks - 1, 1)
    ramp_rows = 1.0 + 2.0 * row_pos
    factor = jnp.exp(jax.random.uniform(key, (row_blocks, col_blocks), jnp.float32, math.log(1.0 / 3.0), math.log(3.0)))
    return factor * ramp_rows[:, None] / (73.0 * math.sqrt(NCELL))


def draw_depth_weight(key, part):
    key = jax.random.fold_in(key, 3)
    cell_pos = jnp.arange(NCELL, dtype=jnp.float32) / max(NCELL - 1, 1)
    rough = jnp.exp(jax.random.uniform(key, (NCELL,), jnp.float32, math.log(0.7), math.log(1.5)))
    return jnp.exp(-math.log(3.0) * cell_pos) * rough


def level_of(rng, dims, pieces, low, largest):
    def one(position, blocks):
        draws = jax.random.uniform(jax.random.fold_in(jax.random.fold_in(rng, 6), position), (blocks,), jnp.float32, low / len(pieces), largest / len(pieces))
        return jnp.repeat(jnp.exp(draws), dims[position] // blocks).reshape((-1,) + (1,) * (len(dims) - position - 1))

    level = one(*pieces[0])
    for cut in pieces[1:]:
        level = level * one(*cut)
    return level


def noise(rng, shape, deviation, reach, split=(), kind=jnp.bfloat16):
    drawn = deviation * jax.random.normal(rng, shape, jnp.float32)
    if split:
        drawn = drawn * level_of(rng, shape, split, -0.22, 0.18)
    return jnp.clip(drawn, -reach, reach).astype(kind)


def setup_inputs(seed: int = 0, part: int = 0) -> dict:
    key_list = jax.random.split(jax.random.key(seed), 8)
    part_splits = jax.random.split(jax.random.fold_in(key_list[7], part), 8)
    sensitivity = draw_sensitivity(jax.random.fold_in(jax.random.fold_in(key_list[7], part), 71), part)
    block_scale = draw_block_scale(jax.random.fold_in(jax.random.fold_in(key_list[7], part), 71), part)
    depth_weight = draw_depth_weight(jax.random.fold_in(jax.random.fold_in(key_list[7], part), 71), part)
    model = noise(part_splits[3], (NSETS, NCELL), 1.0, 6.0, ((1, 8),), jnp.float32)
    residual = noise(part_splits[4], (NSETS, NDATA), 1.0, 6.0, ((1, 2),), jnp.float32)
    direction = noise(part_splits[5], (NSETS, NCELL), 0.5, 3.0, ((1, 8),), jnp.float32)
    gamma = jnp.clip(jnp.exp(jax.random.uniform(part_splits[6], (NSETS,), jnp.float32, math.log(8192.0), math.log(32768.0))), 8192.0, 32768.0)
    return {"sensitivity": sensitivity, "block_scale": block_scale, "depth_weight": depth_weight, "model": model, "residual": residual, "direction": direction, "gamma": gamma}


EPSILON = 1e-6


def reference(sensitivity, block_scale, depth_weight, model, residual, direction, gamma):
    row_blocks = NDATA // BLOCK
    col_blocks = CELLS_DEV // BLOCK
    slab_count = NCELL // CELLS_DEV
    scaled = (direction / depth_weight[None, :]).astype(jnp.bfloat16)
    slab_ids = jnp.arange(slab_count, dtype=jnp.int32)

    def slab_parts(slab_idx):
        begin = (slab_idx * CELLS_DEV).astype(jnp.int32)
        sens_slab = lax.dynamic_slice_in_dim(sensitivity, begin, CELLS_DEV, 1).astype(jnp.float32)
        sens_slab = sens_slab.reshape(row_blocks, BLOCK, col_blocks, BLOCK)
        scale_slab = lax.dynamic_slice_in_dim(block_scale, (slab_idx * col_blocks).astype(jnp.int32), col_blocks, 1)
        return begin, sens_slab, scale_slab

    def predict(total, slab_idx):
        begin, sens_slab, scale_slab = slab_parts(slab_idx)
        vec_slab = lax.dynamic_slice_in_dim(scaled, begin, CELLS_DEV, 1).astype(jnp.float32)
        vec_slab = vec_slab.reshape(NSETS, col_blocks, BLOCK)
        tile_sums = jnp.einsum("aibj,kbj->kabi", sens_slab, vec_slab, precision=lax.Precision.HIGHEST)
        part_sum = jnp.sum(tile_sums * scale_slab[None, :, :, None], axis=2).reshape(NSETS, NDATA)
        return total + part_sum, None

    predicted, _ = lax.scan(predict, jnp.zeros((NSETS, NDATA), jnp.float32), slab_ids)
    curvature = jnp.sum(predicted * predicted, axis=1)
    step_len = gamma / (curvature + EPSILON)
    model_new = model + step_len[:, None] * direction
    residual_new = residual - step_len[:, None] * predicted
    weighted = residual_new.astype(jnp.bfloat16).astype(jnp.float32).reshape(NSETS, row_blocks, BLOCK)

    def backward(slab_idx):
        begin, sens_slab, scale_slab = slab_parts(slab_idx)
        back_tiles = jnp.einsum("aibj,kai->kabj", sens_slab, weighted, precision=lax.Precision.HIGHEST)
        return jnp.sum(back_tiles * scale_slab[None, :, :, None], axis=1).reshape(NSETS, CELLS_DEV)

    slabs = lax.map(backward, slab_ids)
    gradient = jnp.transpose(slabs, (1, 0, 2)).reshape(NSETS, NCELL) / depth_weight[None, :]
    gamma_new = jnp.sum(gradient * gradient, axis=1)
    direction_new = gradient + (gamma_new / gamma)[:, None] * direction
    return model_new, residual_new, direction_new, gamma_new
```

```python
import functools

import jax
import jax.numpy as jnp
from jax import lax
from jax.experimental import pallas as pl
from jax.experimental.pallas import tpu as pltpu
from jax.sharding import PartitionSpec as P

EPSILON = 1e-06
BLOCK = 128
MESH = pl.DeviceIdType.MESH


def to_row(column, first):
    shape = (column.shape[0], 128)
    place = lax.broadcasted_iota(jnp.int32, shape, 0) + first
    lane = lax.broadcasted_iota(jnp.int32, shape, 1)
    return jnp.sum(jnp.where(place == lane, column, 0.0), axis=0, keepdims=True)


def to_column(row, count):
    shape = (count, 128)
    place = lax.broadcasted_iota(jnp.int32, shape, 0)
    lane = lax.broadcasted_iota(jnp.int32, shape, 1)
    return jnp.sum(jnp.where(place == lane, row, 0.0), axis=1, keepdims=True)


def kernel(
    n, nr, ns,
    sens_hbm, scale, depth, model_hbm, resid_hbm, direc_hbm, gamma,
    model_out, resid_out, direc_out, gamma_out,
    sens, model, resid, direc, scaled, part, recv, pred, curv, grad, other, gams,
    sens_sem, load_sem, out_sem,
    rs_send, rs_recv, ag_send, ag_recv, cv_send, cv_recv, dp_send, dp_recv, gm_send, gm_recv,
):
    sets, cells = direc.shape
    cs, cr = recv.shape[1:]
    row_blocks = cr // BLOCK
    col_blocks = cells // BLOCK
    pieces = grad.shape[0]
    width = grad.shape[2]
    total = 2 * n
    me = lax.axis_index("cell")
    core = lax.axis_index("dp")
    rank = me * 2 + core
    my_q = me // ns
    my_g = me % ns

    def sens_copy(t):
        q = lax.rem(my_q + 1 + t, nr)
        return pltpu.make_async_copy(
            sens_hbm.at[pl.ds(pl.multiple_of(q * cr, cr), cr), :], sens.at[t], sens_sem.at[t]
        )

    direc_load = pltpu.make_async_copy(direc_hbm, direc, load_sem.at[0])
    direc_load.start()
    for t in range(nr):
        sens_copy(t).start()
    resid_load = pltpu.make_async_copy(resid_hbm, resid, load_sem.at[1])
    resid_load.start()
    model_load = pltpu.make_async_copy(model_hbm, model, load_sem.at[2])
    model_load.start()

    barrier = pltpu.get_barrier_semaphore()

    def greet(t, _):
        peer = lax.rem(rank + t, total)
        pl.semaphore_signal(
            barrier, inc=1, device_id={"cell": peer // 2, "dp": lax.rem(peer, 2)}, device_id_type=MESH
        )
        return 0

    lax.fori_loop(1, total, greet, 0)

    inverse = 1.0 / depth[...].reshape(1, cells)
    gamma_row = jnp.concatenate(
        [gamma[...].reshape(1, sets), jnp.ones((1, 128 - sets), jnp.float32)], axis=1
    )
    direc_load.wait()
    scaled[...] = (direc[...] * inverse).astype(jnp.bfloat16)
    pl.semaphore_wait(barrier, total - 1)

    def rs_copy(q, g):
        j = q * ns + g
        return pltpu.make_async_remote_copy(
            src_ref=part.at[q, pl.ds(pl.multiple_of(g * cs, cs), cs), :],
            dst_ref=recv.at[me],
            send_sem=rs_send.at[j],
            recv_sem=rs_recv.at[me],
            device_id={"cell": j},
            device_id_type=MESH,
        )

    def forward(t, _):
        q = lax.rem(my_q + 1 + t, nr)
        sens_copy(t).wait()
        accs = [None] * row_blocks
        for b in range(col_blocks):
            tile = lax.dot_general(
                scaled[:, b * BLOCK:(b + 1) * BLOCK],
                sens[t, :, b * BLOCK:(b + 1) * BLOCK],
                (((1,), (1,)), ((), ())),
                preferred_element_type=jnp.float32,
            )
            for a in range(row_blocks):
                term = tile[:, a * BLOCK:(a + 1) * BLOCK] * scale[q * row_blocks + a, b]
                accs[a] = term if accs[a] is None else accs[a] + term
        for a in range(row_blocks):
            part[q, :, a * BLOCK:(a + 1) * BLOCK] = accs[a]

        def send(g, _):
            @pl.when(q * ns + g != me)
            def _():
                rs_copy(q, g).start()
            return 0

        lax.fori_loop(0, ns, send, 0)
        return 0

    lax.fori_loop(0, nr, forward, 0)

    mine = pl.ds(pl.multiple_of(my_g * cs, cs), cs)

    def rs_arrival(src):
        return pltpu.make_async_remote_copy(
            src_ref=recv.at[src], dst_ref=recv.at[src], send_sem=rs_send.at[src],
            recv_sem=rs_recv.at[src], device_id={"cell": src}, device_id_type=MESH,
        )

    pred[my_q, mine, :] = part[my_q, mine, :]

    def reduce(t, _):
        src = lax.rem(me + t, n)
        rs_arrival(src).wait_recv()
        pred[my_q, mine, :] += recv[src]
        return 0

    lax.fori_loop(1, n, reduce, 0)

    value = pred[my_q, mine, :]
    curv[rank] = to_row(jnp.sum(value * value, axis=1, keepdims=True), my_g * cs)

    def cv_copy(slot, peer):
        return pltpu.make_async_remote_copy(
            src_ref=curv.at[slot], dst_ref=curv.at[slot], send_sem=cv_send.at[peer],
            recv_sem=cv_recv.at[slot],
            device_id={"cell": peer // 2, "dp": lax.rem(peer, 2)}, device_id_type=MESH,
        )

    def cv_start(t, _):
        cv_copy(rank, lax.rem(rank + t, total)).start()
        return 0

    lax.fori_loop(1, total, cv_start, 0)

    def ag_copy(q, g, peer):
        ref = pred.at[q, pl.ds(pl.multiple_of(g * cs, cs), cs), :]
        return pltpu.make_async_remote_copy(
            src_ref=ref, dst_ref=ref, send_sem=ag_send.at[peer],
            recv_sem=ag_recv.at[q * ns + g], device_id={"cell": peer}, device_id_type=MESH,
        )

    def ag_start(t, _):
        ag_copy(my_q, my_g, lax.rem(me + t, n)).start()
        return 0

    lax.fori_loop(1, n, ag_start, 0)

    def cv_wait(t, _):
        peer = lax.rem(rank + t, total)
        cv_copy(peer, peer).wait_recv()
        return 0

    lax.fori_loop(1, total, cv_wait, 0)
    curvature = lax.fori_loop(
        0, total, lambda i, acc: acc + curv[i], jnp.zeros((1, 128), jnp.float32)
    )
    step = to_column(gamma_row / (curvature + EPSILON), sets)

    model_load.wait()
    model[...] = model[...] + step * direc[...]
    model_store = pltpu.make_async_copy(model, model_out, out_sem.at[0])
    model_store.start()
    resid_load.wait()
    grad[...] = jnp.zeros(grad.shape, jnp.float32)

    def backward(u, _):
        t = nr - 1 - u
        q = lax.rem(my_q + 1 + t, nr)

        def arrive(g, _):
            @pl.when(q * ns + g != me)
            def _():
                ag_copy(q, g, q * ns + g).wait_recv()
            return 0

        lax.fori_loop(0, ns, arrive, 0)
        where = pl.ds(pl.multiple_of(q * cr, cr), cr)
        fresh = resid[:, where] - step * pred[q]
        resid[:, where] = fresh
        weighted = fresh.astype(jnp.bfloat16)
        for p in range(pieces):
            acc = grad[p]
            for a in range(row_blocks):
                tile = jnp.dot(
                    weighted[:, a * BLOCK:(a + 1) * BLOCK],
                    sens[t, a * BLOCK:(a + 1) * BLOCK, p * width:(p + 1) * width],
                    preferred_element_type=jnp.float32,
                )
                acc = acc + jnp.concatenate(
                    [
                        tile[:, b * BLOCK:(b + 1) * BLOCK]
                        * scale[q * row_blocks + a, p * (width // BLOCK) + b]
                        for b in range(width // BLOCK)
                    ],
                    axis=1,
                )
            grad[p] = acc
        return 0

    lax.fori_loop(0, nr, backward, 0)

    def dp_copy(p):
        return pltpu.make_async_remote_copy(
            src_ref=grad.at[p], dst_ref=other.at[p], send_sem=dp_send.at[p],
            recv_sem=dp_recv.at[p], device_id={"dp": 1 - core}, device_id_type=MESH,
        )

    for p in range(pieces):
        dp_copy(p).start()
    resid_store = pltpu.make_async_copy(resid, resid_out, out_sem.at[1])
    resid_store.start()

    square = jnp.zeros((sets, 1), jnp.float32)
    for p in range(pieces):
        dp_copy(p).wait()
        full = (grad[p] + other[p]) * inverse[:, p * width:(p + 1) * width]
        grad[p] = full
        square = square + jnp.sum(full * full, axis=1, keepdims=True)
    gams[me] = to_row(square, 0)

    def gm_copy(slot, peer):
        return pltpu.make_async_remote_copy(
            src_ref=gams.at[slot], dst_ref=gams.at[slot], send_sem=gm_send.at[peer],
            recv_sem=gm_recv.at[slot], device_id={"cell": peer}, device_id_type=MESH,
        )

    def gm_start(t, _):
        gm_copy(me, lax.rem(me + t, n)).start()
        return 0

    def gm_wait(t, _):
        peer = lax.rem(me + t, n)
        gm_copy(peer, peer).wait_recv()
        return 0

    lax.fori_loop(1, n, gm_start, 0)
    lax.fori_loop(1, n, gm_wait, 0)
    gamma_new = lax.fori_loop(
        0, n, lambda i, acc: acc + gams[i], jnp.zeros((1, 128), jnp.float32)
    )
    gamma_out[...] = gamma_new[:, :sets].reshape(sets)
    ratio = to_column(gamma_new / gamma_row, sets)
    for p in range(pieces):
        span = slice(p * width, (p + 1) * width)
        direc[:, span] = grad[p] + ratio * direc[:, span]
    direc_store = pltpu.make_async_copy(direc, direc_out, out_sem.at[2])
    direc_store.start()

    def drain(t, _):
        peer = lax.rem(me + t, n)
        rs_arrival(peer).wait_send()
        ag_copy(my_q, my_g, peer).wait_send()
        gm_copy(me, peer).wait_send()
        return 0

    def cv_drain(t, _):
        cv_copy(rank, lax.rem(rank + t, total)).wait_send()
        return 0

    lax.fori_loop(1, n, drain, 0)
    lax.fori_loop(1, total, cv_drain, 0)
    model_store.wait()
    resid_store.wait()
    direc_store.wait()


def local(n, sensitivity, block_scale, depth_weight, model, residual, direction, gamma):
    rows, cells = sensitivity.shape
    sets = direction.shape[0]
    nr = min(n, rows // BLOCK)
    ns = n // nr
    cr, cs = rows // nr, sets // ns
    pieces = 4
    f32 = jnp.float32
    any_space = pl.BlockSpec(memory_space=pl.ANY)
    vmem = pl.BlockSpec(memory_space=pltpu.VMEM)
    smem = pl.BlockSpec(memory_space=pltpu.SMEM)
    dma = pltpu.SemaphoreType.DMA
    return pl.pallas_call(
        functools.partial(kernel, n, nr, ns),
        out_shape=(
            jax.ShapeDtypeStruct(model.shape, f32),
            jax.ShapeDtypeStruct(residual.shape, f32),
            jax.ShapeDtypeStruct(direction.shape, f32),
            jax.ShapeDtypeStruct(gamma.shape, f32),
        ),
        in_specs=[any_space, smem, vmem, any_space, any_space, any_space, vmem],
        out_specs=(any_space, any_space, any_space, vmem),
        scratch_shapes=[
            pltpu.VMEM((nr, cr, cells), jnp.bfloat16),
            pltpu.VMEM((sets, cells), f32),
            pltpu.VMEM((sets, rows), f32),
            pltpu.VMEM((sets, cells), f32),
            pltpu.VMEM((sets, cells), jnp.bfloat16),
            pltpu.VMEM((nr, sets, cr), f32),
            pltpu.VMEM((n, cs, cr), f32),
            pltpu.VMEM((nr, sets, cr), f32),
            pltpu.VMEM((2 * n, 1, 128), f32),
            pltpu.VMEM((pieces, sets, cells // pieces), f32),
            pltpu.VMEM((pieces, sets, cells // pieces), f32),
            pltpu.VMEM((n, 1, 128), f32),
            dma((nr,)), dma((3,)), dma((3,)),
            dma((n,)), dma((n,)), dma((n,)), dma((n,)),
            dma((2 * n,)), dma((2 * n,)), dma((pieces,)), dma((pieces,)),
            dma((n,)), dma((n,)),
        ],
        compiler_params=pltpu.CompilerParams(
            collective_id=0, has_side_effects=True, vmem_limit_bytes=32 * 1024 * 1024
        ),
        cost_estimate=pl.CostEstimate(
            flops=4 * rows * cells * sets, bytes_accessed=2 * rows * cells, transcendentals=0
        ),
        name="cgls_iteration",
    )(sensitivity, block_scale, depth_weight, model, residual, direction, gamma)


def solution(mesh):
    in_specs = (
        P(("groups", "dp"), "cell"),
        P(("groups", "dp"), "cell"),
        P(("groups", "cell")),
        P("groups", "cell"),
        P("groups", "dp"),
        P("groups", "cell"),
        P("groups"),
    )
    out_specs = (P("groups", "cell"), P("groups", "dp"), P("groups", "cell"), P("groups"))
    return jax.shard_map(
        functools.partial(local, mesh.shape["cell"]),
        mesh=mesh, in_specs=in_specs, out_specs=out_specs, check_vma=False,
    )
```

```python
import functools

import jax
import jax.numpy as jnp
from jax import lax
from jax.experimental import pallas as pl
from jax.experimental.pallas import tpu as pltpu
from jax.sharding import PartitionSpec as P

EPSILON = 1e-06
BLOCK = 128
MESH = pl.DeviceIdType.MESH


def to_row(column, first):
    shape = (column.shape[0], 128)
    place = lax.broadcasted_iota(jnp.int32, shape, 0) + first
    lane = lax.broadcasted_iota(jnp.int32, shape, 1)
    return jnp.sum(jnp.where(place == lane, column, 0.0), axis=0, keepdims=True)


def to_column(row, count):
    shape = (count, 128)
    place = lax.broadcasted_iota(jnp.int32, shape, 0)
    lane = lax.broadcasted_iota(jnp.int32, shape, 1)
    return jnp.sum(jnp.where(place == lane, row, 0.0), axis=1, keepdims=True)


def kernel(
    n, nr, ns,
    sens_hbm, scale_hbm, depth_hbm, model_hbm, resid_hbm, direc_hbm, gamma_hbm,
    model, resid, direc, grad, small,
    scale, depth, gamma, sens, scaled, part, recv, pred, curv, other, gams,
    sens_sem, load_sem,
    rs_send, rs_recv, ag_send, ag_recv, cv_send, cv_recv, dp_send, dp_recv, gm_send, gm_recv,
):
    sets, cells = direc.shape
    cs, cr = recv.shape[1:]
    row_blocks = cr // BLOCK
    col_blocks = cells // BLOCK
    pieces = grad.shape[0]
    width = grad.shape[2]
    total = 2 * n
    me = lax.axis_index("cell")
    core = lax.axis_index("dp")
    rank = me * 2 + core
    my_q = me // ns
    my_g = me % ns

    def sens_copy(t):
        q = lax.rem(my_q + 1 + t, nr)
        return pltpu.make_async_copy(
            sens_hbm.at[pl.ds(pl.multiple_of(q * cr, cr), cr), :], sens.at[t], sens_sem.at[t]
        )

    direc_load = pltpu.make_async_copy(direc_hbm, direc, load_sem.at[0])
    direc_load.start()
    depth_load = pltpu.make_async_copy(depth_hbm, depth, load_sem.at[3])
    depth_load.start()
    scale_load = pltpu.make_async_copy(scale_hbm, scale, load_sem.at[4])
    scale_load.start()
    gamma_load = pltpu.make_async_copy(gamma_hbm, gamma, load_sem.at[5])
    gamma_load.start()
    for t in range(nr):
        sens_copy(t).start()
    resid_load = pltpu.make_async_copy(resid_hbm, resid, load_sem.at[1])
    resid_load.start()
    model_load = pltpu.make_async_copy(model_hbm, model, load_sem.at[2])
    model_load.start()

    barrier = pltpu.get_barrier_semaphore()

    def greet(t, _):
        peer = lax.rem(rank + t, total)
        pl.semaphore_signal(
            barrier, inc=1, device_id={"cell": peer // 2, "dp": lax.rem(peer, 2)}, device_id_type=MESH
        )
        return 0

    lax.fori_loop(1, total, greet, 0)

    depth_load.wait()
    gamma_load.wait()
    scale_load.wait()
    inverse = 1.0 / depth[...].reshape(1, cells)
    gamma_row = jnp.concatenate(
        [gamma[...].reshape(1, sets), jnp.ones((1, 128 - sets), jnp.float32)], axis=1
    )
    direc_load.wait()
    scaled[...] = (direc[...] * inverse).astype(jnp.bfloat16)
    pl.semaphore_wait(barrier, total - 1)

    def rs_copy(q, g):
        j = q * ns + g
        return pltpu.make_async_remote_copy(
            src_ref=part.at[q, pl.ds(pl.multiple_of(g * cs, cs), cs), :],
            dst_ref=recv.at[me],
            send_sem=rs_send.at[j],
            recv_sem=rs_recv.at[me],
            device_id={"cell": j},
            device_id_type=MESH,
        )

    def forward(t, _):
        q = lax.rem(my_q + 1 + t, nr)
        sens_copy(t).wait()
        accs = [None] * row_blocks
        for b in range(col_blocks):
            tile = lax.dot_general(
                scaled[:, b * BLOCK:(b + 1) * BLOCK],
                sens[t, :, b * BLOCK:(b + 1) * BLOCK],
                (((1,), (1,)), ((), ())),
                preferred_element_type=jnp.float32,
            )
            for a in range(row_blocks):
                term = tile[:, a * BLOCK:(a + 1) * BLOCK] * scale[b, q * row_blocks + a]
                accs[a] = term if accs[a] is None else accs[a] + term
        for a in range(row_blocks):
            part[q, :, a * BLOCK:(a + 1) * BLOCK] = accs[a]

        def send(g, _):
            @pl.when(q * ns + g != me)
            def _():
                rs_copy(q, g).start()
            return 0

        lax.fori_loop(0, ns, send, 0)
        return 0

    lax.fori_loop(0, nr, forward, 0)

    mine = pl.ds(pl.multiple_of(my_g * cs, cs), cs)

    def rs_arrival(src):
        return pltpu.make_async_remote_copy(
            src_ref=recv.at[src], dst_ref=recv.at[src], send_sem=rs_send.at[src],
            recv_sem=rs_recv.at[src], device_id={"cell": src}, device_id_type=MESH,
        )

    pred[my_q, mine, :] = part[my_q, mine, :]

    def reduce(t, _):
        src = lax.rem(me + t, n)
        rs_arrival(src).wait_recv()
        pred[my_q, mine, :] += recv[src]
        return 0

    lax.fori_loop(1, n, reduce, 0)

    value = pred[my_q, mine, :]
    curv[rank] = to_row(jnp.sum(value * value, axis=1, keepdims=True), my_g * cs)

    def cv_copy(slot, peer):
        return pltpu.make_async_remote_copy(
            src_ref=curv.at[slot], dst_ref=curv.at[slot], send_sem=cv_send.at[peer],
            recv_sem=cv_recv.at[slot],
            device_id={"cell": peer // 2, "dp": lax.rem(peer, 2)}, device_id_type=MESH,
        )

    def cv_start(t, _):
        cv_copy(rank, lax.rem(rank + t, total)).start()
        return 0

    lax.fori_loop(1, total, cv_start, 0)

    def ag_copy(q, g, peer):
        ref = pred.at[q, pl.ds(pl.multiple_of(g * cs, cs), cs), :]
        return pltpu.make_async_remote_copy(
            src_ref=ref, dst_ref=ref, send_sem=ag_send.at[peer],
            recv_sem=ag_recv.at[q * ns + g], device_id={"cell": peer}, device_id_type=MESH,
        )

    def ag_start(t, _):
        ag_copy(my_q, my_g, lax.rem(me + t, n)).start()
        return 0

    lax.fori_loop(1, n, ag_start, 0)

    def cv_wait(t, _):
        peer = lax.rem(rank + t, total)
        cv_copy(peer, peer).wait_recv()
        return 0

    lax.fori_loop(1, total, cv_wait, 0)
    curvature = lax.fori_loop(
        0, total, lambda i, acc: acc + curv[i], jnp.zeros((1, 128), jnp.float32)
    )
    step = to_column(gamma_row / (curvature + EPSILON), sets)

    model_load.wait()
    model[...] = model[...] + step * direc[...]
    resid_load.wait()
    grad[...] = jnp.zeros(grad.shape, jnp.float32)

    def backward(u, _):
        t = nr - 1 - u
        q = lax.rem(my_q + 1 + t, nr)

        def arrive(g, _):
            @pl.when(q * ns + g != me)
            def _():
                ag_copy(q, g, q * ns + g).wait_recv()
            return 0

        lax.fori_loop(0, ns, arrive, 0)
        where = pl.ds(pl.multiple_of(q * cr, cr), cr)
        fresh = resid[:, where] - step * pred[q]
        resid[:, where] = fresh
        weighted = fresh.astype(jnp.bfloat16)
        for p in range(pieces):
            acc = grad[p]
            for a in range(row_blocks):
                tile = jnp.dot(
                    weighted[:, a * BLOCK:(a + 1) * BLOCK],
                    sens[t, a * BLOCK:(a + 1) * BLOCK, p * width:(p + 1) * width],
                    preferred_element_type=jnp.float32,
                )
                acc = acc + jnp.concatenate(
                    [
                        tile[:, b * BLOCK:(b + 1) * BLOCK]
                        * scale[p * (width // BLOCK) + b, q * row_blocks + a]
                        for b in range(width // BLOCK)
                    ],
                    axis=1,
                )
            grad[p] = acc
        return 0

    lax.fori_loop(0, nr, backward, 0)

    def dp_copy(p):
        return pltpu.make_async_remote_copy(
            src_ref=grad.at[p], dst_ref=other.at[p], send_sem=dp_send.at[p],
            recv_sem=dp_recv.at[p], device_id={"dp": 1 - core}, device_id_type=MESH,
        )

    for p in range(pieces):
        dp_copy(p).start()

    square = jnp.zeros((sets, 1), jnp.float32)
    for p in range(pieces):
        dp_copy(p).wait()
        full = (grad[p] + other[p]) * inverse[:, p * width:(p + 1) * width]
        grad[p] = full
        square = square + jnp.sum(full * full, axis=1, keepdims=True)
    gams[me] = to_row(square, 0)

    def gm_copy(slot, peer):
        return pltpu.make_async_remote_copy(
            src_ref=gams.at[slot], dst_ref=gams.at[slot], send_sem=gm_send.at[peer],
            recv_sem=gm_recv.at[slot], device_id={"cell": peer}, device_id_type=MESH,
        )

    def gm_start(t, _):
        gm_copy(me, lax.rem(me + t, n)).start()
        return 0

    def gm_wait(t, _):
        peer = lax.rem(me + t, n)
        gm_copy(peer, peer).wait_recv()
        return 0

    lax.fori_loop(1, n, gm_start, 0)
    lax.fori_loop(1, n, gm_wait, 0)
    gamma_new = lax.fori_loop(
        0, n, lambda i, acc: acc + gams[i], jnp.zeros((1, 128), jnp.float32)
    )
    small[0:1, :] = gamma_new
    small[1:2, :] = gamma_new / gamma_row

    def drain(t, _):
        peer = lax.rem(me + t, n)
        rs_arrival(peer).wait_send()
        ag_copy(my_q, my_g, peer).wait_send()
        gm_copy(me, peer).wait_send()
        return 0

    def cv_drain(t, _):
        cv_copy(rank, lax.rem(rank + t, total)).wait_send()
        return 0

    lax.fori_loop(1, n, drain, 0)
    lax.fori_loop(1, total, cv_drain, 0)


def finish(model, resid, direc, grad, small, model_out, resid_out, direc_out, gamma_out, fresh, sem):
    sets = direc.shape[0]
    pieces, _, width = grad.shape
    copies = [
        pltpu.make_async_copy(model, model_out, sem.at[0]),
        pltpu.make_async_copy(resid, resid_out, sem.at[1]),
    ]
    for copy in copies:
        copy.start()
    ratio = to_column(small[1:2, :], sets)
    for p in range(pieces):
        span = slice(p * width, (p + 1) * width)
        fresh[:, span] = grad[p] + ratio * direc[:, span]
    last = pltpu.make_async_copy(fresh, direc_out, sem.at[2])
    last.start()
    gamma_out[...] = small[0, :sets]
    for copy in copies:
        copy.wait()
    last.wait()


def local(n, sensitivity, block_scale, depth_weight, model, residual, direction, gamma):
    rows, cells = sensitivity.shape
    sets = direction.shape[0]
    nr = min(n, rows // BLOCK)
    ns = n // nr
    cr, cs = rows // nr, sets // ns
    pieces = 4
    f32 = jnp.float32
    hbm = pl.BlockSpec(memory_space=pltpu.HBM)
    vmem = pl.BlockSpec(memory_space=pltpu.VMEM)
    dma = pltpu.SemaphoreType.DMA
    parts = pl.pallas_call(
        functools.partial(kernel, n, nr, ns),
        out_shape=(
            pltpu.VMEM(model.shape, f32),
            pltpu.VMEM(residual.shape, f32),
            pltpu.VMEM(direction.shape, f32),
            pltpu.VMEM((pieces, sets, cells // pieces), f32),
            pltpu.VMEM((8, 128), f32),
        ),
        in_specs=[hbm] * 7,
        out_specs=(vmem,) * 5,
        scratch_shapes=[
            pltpu.SMEM(block_scale.shape[::-1], f32),
            pltpu.VMEM(depth_weight.shape, f32),
            pltpu.VMEM(gamma.shape, f32),
            pltpu.VMEM((nr, cr, cells), jnp.bfloat16),
            pltpu.VMEM((sets, cells), jnp.bfloat16),
            pltpu.VMEM((nr, sets, cr), f32),
            pltpu.VMEM((n, cs, cr), f32),
            pltpu.VMEM((nr, sets, cr), f32),
            pltpu.VMEM((2 * n, 1, 128), f32),
            pltpu.VMEM((pieces, sets, cells // pieces), f32),
            pltpu.VMEM((n, 1, 128), f32),
            dma((nr,)), dma((6,)),
            dma((n,)), dma((n,)), dma((n,)), dma((n,)),
            dma((2 * n,)), dma((2 * n,)), dma((pieces,)), dma((pieces,)),
            dma((n,)), dma((n,)),
        ],
        compiler_params=pltpu.CompilerParams(
            collective_id=0, has_side_effects=True, vmem_limit_bytes=56 * 1024 * 1024
        ),
        cost_estimate=pl.CostEstimate(
            flops=4 * rows * cells * sets, bytes_accessed=2 * rows * cells, transcendentals=0
        ),
        name="cgls_iteration",
    )(sensitivity, block_scale.T, depth_weight, model, residual, direction, gamma)
    return pl.pallas_call(
        finish,
        out_shape=(
            jax.ShapeDtypeStruct(model.shape, f32),
            jax.ShapeDtypeStruct(residual.shape, f32),
            jax.ShapeDtypeStruct(direction.shape, f32),
            jax.ShapeDtypeStruct(gamma.shape, f32),
        ),
        in_specs=[vmem] * 5,
        out_specs=(hbm, hbm, hbm, vmem),
        scratch_shapes=[pltpu.VMEM(direction.shape, f32), dma((3,))],
        compiler_params=pltpu.CompilerParams(vmem_limit_bytes=16 * 1024 * 1024),
        name="cgls_results",
    )(*parts)


def solution(mesh):
    in_specs = (
        P(("groups", "dp"), "cell"),
        P(("groups", "dp"), "cell"),
        P(("groups", "cell")),
        P("groups", "cell"),
        P("groups", "dp"),
        P("groups", "cell"),
        P("groups"),
    )
    out_specs = (P("groups", "cell"), P("groups", "dp"), P("groups", "cell"), P("groups"))
    return jax.shard_map(
        functools.partial(local, mesh.shape["cell"]),
        mesh=mesh, in_specs=in_specs, out_specs=out_specs, check_vma=False,
    )
```

```python
import functools

import jax
import jax.numpy as jnp
from jax import lax
from jax.experimental import pallas as pl
from jax.experimental.pallas import tpu as pltpu
from jax.sharding import PartitionSpec as P

EPSILON = 1e-06
BLOCK = 128
MESH = pl.DeviceIdType.MESH


def to_row(column, first):
    shape = (column.shape[0], 128)
    place = lax.broadcasted_iota(jnp.int32, shape, 0) + first
    lane = lax.broadcasted_iota(jnp.int32, shape, 1)
    return jnp.sum(jnp.where(place == lane, column, 0.0), axis=0, keepdims=True)


def to_column(row, count):
    shape = (count, 128)
    place = lax.broadcasted_iota(jnp.int32, shape, 0)
    lane = lax.broadcasted_iota(jnp.int32, shape, 1)
    return jnp.sum(jnp.where(place == lane, row, 0.0), axis=1, keepdims=True)


def kernel(
    n, nr, ns, fa, ga,
    sens_hbm, scale_hbm, depth_hbm, model_hbm, resid_hbm, direc_hbm, gamma_hbm,
    model, resid, direc, grad, small,
    scale, depth, gamma, sens, scaled, part, recv, xin, zin, pred, curv, other, gams,
    sens_sem, load_sem, x_send, x_recv, z_send, z_recv, ax_send, ax_recv, az_send, az_recv,
    rs_send, rs_recv, ag_send, ag_recv, cv_send, cv_recv, dp_send, dp_recv, gm_send, gm_recv,
):
    sets, cells = direc.shape
    cs, cr = sets // ns, recv.shape[2]
    paired = fa > 0
    nz = n // 2
    row_blocks = cr // BLOCK
    col_blocks = cells // BLOCK
    pieces = grad.shape[0]
    width = grad.shape[2]
    total = 2 * n
    me = lax.axis_index("cell")
    core = lax.axis_index("dp")
    rank = me * 2 + core
    my_q = me // ns
    my_g = me % ns
    x = lax.rem(me, 2)
    z = me // 2
    beside = 2 * z + 1 - x

    def chunk_at(t):
        if not paired:
            return lax.rem(my_q + 1 + t, nr)
        return 2 * lax.rem(z + 1 + t, nz) + lax.rem(x + 1 + t // nz, 2)

    def sens_copy(t):
        q = chunk_at(t)
        return pltpu.make_async_copy(
            sens_hbm.at[pl.ds(pl.multiple_of(q * cr, cr), cr), :], sens.at[t], sens_sem.at[t]
        )

    direc_load = pltpu.make_async_copy(direc_hbm, direc, load_sem.at[0])
    direc_load.start()
    depth_load = pltpu.make_async_copy(depth_hbm, depth, load_sem.at[3])
    depth_load.start()
    scale_load = pltpu.make_async_copy(scale_hbm, scale, load_sem.at[4])
    scale_load.start()
    gamma_load = pltpu.make_async_copy(gamma_hbm, gamma, load_sem.at[5])
    gamma_load.start()
    for t in range(nr):
        sens_copy(t).start()
    resid_load = pltpu.make_async_copy(resid_hbm, resid, load_sem.at[1])
    resid_load.start()
    model_load = pltpu.make_async_copy(model_hbm, model, load_sem.at[2])
    model_load.start()

    barrier = pltpu.get_barrier_semaphore()

    def greet(t, _):
        peer = lax.rem(rank + t, total)
        pl.semaphore_signal(
            barrier, inc=1, device_id={"cell": peer // 2, "dp": lax.rem(peer, 2)}, device_id_type=MESH
        )
        return 0

    lax.fori_loop(1, total, greet, 0)

    depth_load.wait()
    gamma_load.wait()
    scale_load.wait()
    inverse = 1.0 / depth[...].reshape(1, cells)
    gamma_row = jnp.concatenate(
        [gamma[...].reshape(1, sets), jnp.ones((1, 128 - sets), jnp.float32)], axis=1
    )
    direc_load.wait()
    scaled[...] = (direc[...] * inverse).astype(jnp.bfloat16)
    pl.semaphore_wait(barrier, total - 1)

    def rs_copy(q, g):
        j = q * ns + g
        return pltpu.make_async_remote_copy(
            src_ref=part.at[q, pl.ds(pl.multiple_of(g * cs + fa, 8), cs - fa), :],
            dst_ref=recv.at[me],
            send_sem=rs_send.at[j],
            recv_sem=rs_recv.at[me],
            device_id={"cell": j},
            device_id_type=MESH,
        )

    def forward(t):
        q = chunk_at(t)
        sens_copy(t).wait()
        accs = [None] * row_blocks
        for b in range(col_blocks):
            tile = lax.dot_general(
                scaled[:, b * BLOCK:(b + 1) * BLOCK],
                sens[t, :, b * BLOCK:(b + 1) * BLOCK],
                (((1,), (1,)), ((), ())),
                preferred_element_type=jnp.float32,
            )
            for a in range(row_blocks):
                term = tile[:, a * BLOCK:(a + 1) * BLOCK] * scale[b, q * row_blocks + a]
                accs[a] = term if accs[a] is None else accs[a] + term
        for a in range(row_blocks):
            part[q, :, a * BLOCK:(a + 1) * BLOCK] = accs[a]
        return q

    def x_copy(zz):
        return pltpu.make_async_remote_copy(
            src_ref=part.at[2 * zz + 1 - x, pl.ds(0, fa), :], dst_ref=xin.at[zz],
            send_sem=x_send.at[zz], recv_sem=x_recv.at[zz],
            device_id={"cell": beside}, device_id_type=MESH,
        )

    def z_copy(slot, zz):
        return pltpu.make_async_remote_copy(
            src_ref=part.at[2 * zz + x, pl.ds(0, fa), :], dst_ref=zin.at[slot],
            send_sem=z_send.at[zz], recv_sem=z_recv.at[slot],
            device_id={"cell": 2 * zz + x}, device_id_type=MESH,
        )

    if paired:
        def across(t, _):
            q = forward(t)
            x_copy(q // 2).start()
            rs_copy(q, 0).start()
            return 0

        def along(t, _):
            rs_copy(forward(t), 0).start()
            return 0

        def pass_on(t, _):
            zz = lax.rem(z + 1 + t, nz)
            x_copy(zz).wait_recv()
            part[2 * zz + x, :fa, :] += xin[zz]
            z_copy(z, zz).start()
            return 0

        lax.fori_loop(0, nz, across, 0)
        lax.fori_loop(nz, n - 1, along, 0)
        forward(n - 1)
        lax.fori_loop(0, nz - 1, pass_on, 0)
    else:
        def spread(t, _):
            q = forward(t)

            def send(g, _):
                @pl.when(q * ns + g != me)
                def _():
                    rs_copy(q, g).start()
                return 0

            lax.fori_loop(0, ns, send, 0)
            return 0

        lax.fori_loop(0, nr, spread, 0)

    mine = pl.ds(pl.multiple_of(my_g * cs, 8), cs)
    direct = pl.ds(pl.multiple_of(my_g * cs + fa, 8), cs - fa)

    def rs_arrival(src):
        return pltpu.make_async_remote_copy(
            src_ref=recv.at[src], dst_ref=recv.at[src], send_sem=rs_send.at[src],
            recv_sem=rs_recv.at[src], device_id={"cell": src}, device_id_type=MESH,
        )

    pred[my_q, mine, :] = part[my_q, mine, :]

    def reduce(t, _):
        src = lax.rem(me + t, n)
        rs_arrival(src).wait_recv()
        pred[my_q, direct, :] += recv[src]
        return 0

    lax.fori_loop(1, n, reduce, 0)

    if paired:
        x_copy(z).wait_recv()
        pred[me, :fa, :] += xin[z]

        def reduce_z(t, _):
            zz = lax.rem(z + t, nz)
            z_copy(zz, zz).wait_recv()
            pred[me, :fa, :] += zin[zz]
            return 0

        lax.fori_loop(1, nz, reduce_z, 0)

    value = pred[my_q, mine, :]
    curv[rank] = to_row(jnp.sum(value * value, axis=1, keepdims=True), my_g * cs)

    def cv_copy(slot, peer):
        return pltpu.make_async_remote_copy(
            src_ref=curv.at[slot], dst_ref=curv.at[slot], send_sem=cv_send.at[peer],
            recv_sem=cv_recv.at[slot],
            device_id={"cell": peer // 2, "dp": lax.rem(peer, 2)}, device_id_type=MESH,
        )

    def cv_start(t, _):
        cv_copy(rank, lax.rem(rank + t, total)).start()
        return 0

    lax.fori_loop(1, total, cv_start, 0)

    def ag_copy(q, g, peer):
        ref = pred.at[q, pl.ds(pl.multiple_of(g * cs + ga, 8), cs - ga), :]
        return pltpu.make_async_remote_copy(
            src_ref=ref, dst_ref=ref, send_sem=ag_send.at[peer],
            recv_sem=ag_recv.at[q * ns + g], device_id={"cell": peer}, device_id_type=MESH,
        )

    def az_copy(owner, zz):
        ref = pred.at[owner, pl.ds(0, ga), :]
        return pltpu.make_async_remote_copy(
            src_ref=ref, dst_ref=ref, send_sem=az_send.at[zz], recv_sem=az_recv.at[owner // 2],
            device_id={"cell": 2 * zz + x}, device_id_type=MESH,
        )

    def ax_copy(owner):
        ref = pred.at[owner, pl.ds(0, ga), :]
        return pltpu.make_async_remote_copy(
            src_ref=ref, dst_ref=ref, send_sem=ax_send.at[owner // 2],
            recv_sem=ax_recv.at[owner // 2], device_id={"cell": beside}, device_id_type=MESH,
        )

    if paired:
        for t in range(1, nz):
            az_copy(me, lax.rem(z + t, nz)).start()
        ax_copy(me).start()
        for t in range(1, nz):
            az_copy(me, lax.rem(z + t, nz)).wait_send()
        for t in range(1, nz):
            ag_copy(me, 0, 2 * lax.rem(z + t, nz) + x).start()
        for t in range(nz):
            ag_copy(me, 0, 2 * lax.rem(z + t, nz) + 1 - x).start()
        for t in range(1, nz):
            zz = lax.rem(z + nz - t, nz)
            az_copy(2 * zz + x, zz).wait_recv()
            ax_copy(2 * zz + x).start()
    else:
        def ag_start(t, _):
            ag_copy(my_q, my_g, lax.rem(me + t, n)).start()
            return 0

        lax.fori_loop(1, n, ag_start, 0)

    def cv_wait(t, _):
        peer = lax.rem(rank + t, total)
        cv_copy(peer, peer).wait_recv()
        return 0

    lax.fori_loop(1, total, cv_wait, 0)
    curvature = lax.fori_loop(
        0, total, lambda i, acc: acc + curv[i], jnp.zeros((1, 128), jnp.float32)
    )
    step = to_column(gamma_row / (curvature + EPSILON), sets)

    model_load.wait()
    model[...] = model[...] + step * direc[...]
    resid_load.wait()
    grad[...] = jnp.zeros(grad.shape, jnp.float32)

    def dp_copy(p):
        return pltpu.make_async_remote_copy(
            src_ref=grad.at[p], dst_ref=other.at[p], send_sem=dp_send.at[p],
            recv_sem=dp_recv.at[p], device_id={"dp": 1 - core}, device_id_type=MESH,
        )

    def backward(t, last):
        q = chunk_at(t)

        def arrive(g, _):
            @pl.when(q * ns + g != me)
            def _():
                ag_copy(q, g, q * ns + g).wait_recv()
            return 0

        if not last or not paired:
            lax.fori_loop(0, ns, arrive, 0)
        else:
            ag_copy(q, 0, q).wait_recv()
        where = pl.ds(pl.multiple_of(q * cr, cr), cr)
        fresh = resid[:, where] - step * pred[q]
        resid[:, where] = fresh
        weighted = fresh.astype(jnp.bfloat16)
        for p in range(pieces):
            acc = grad[p]
            for a in range(row_blocks):
                tile = jnp.dot(
                    weighted[:, a * BLOCK:(a + 1) * BLOCK],
                    sens[t, a * BLOCK:(a + 1) * BLOCK, p * width:(p + 1) * width],
                    preferred_element_type=jnp.float32,
                )
                acc = acc + jnp.concatenate(
                    [
                        tile[:, b * BLOCK:(b + 1) * BLOCK]
                        * scale[p * (width // BLOCK) + b, q * row_blocks + a]
                        for b in range(width // BLOCK)
                    ],
                    axis=1,
                )
            grad[p] = acc
            if last:
                dp_copy(p).start()

    def own_column(u, _):
        backward(nr - 1 - u, False)
        return 0

    def other_column(u, _):
        t = nr - 1 - u
        ax_copy(2 * (chunk_at(t) // 2) + x).wait_recv()
        backward(t, False)
        return 0

    if paired:
        lax.fori_loop(0, nz, own_column, 0)
        lax.fori_loop(nz, nr - 1, other_column, 0)
        ax_copy(2 * (chunk_at(0) // 2) + x).wait_recv()
    else:
        lax.fori_loop(0, nr - 1, own_column, 0)
    backward(0, True)

    square = jnp.zeros((sets, 1), jnp.float32)
    for p in range(pieces):
        dp_copy(p).wait()
        full = (grad[p] + other[p]) * inverse[:, p * width:(p + 1) * width]
        grad[p] = full
        square = square + jnp.sum(full * full, axis=1, keepdims=True)
    gams[me] = to_row(square, 0)

    def gm_copy(slot, peer):
        return pltpu.make_async_remote_copy(
            src_ref=gams.at[slot], dst_ref=gams.at[slot], send_sem=gm_send.at[peer],
            recv_sem=gm_recv.at[slot], device_id={"cell": peer}, device_id_type=MESH,
        )

    def gm_start(t, _):
        gm_copy(me, lax.rem(me + t, n)).start()
        return 0

    def gm_wait(t, _):
        peer = lax.rem(me + t, n)
        gm_copy(peer, peer).wait_recv()
        return 0

    lax.fori_loop(1, n, gm_start, 0)
    lax.fori_loop(1, n, gm_wait, 0)
    gamma_new = lax.fori_loop(
        0, n, lambda i, acc: acc + gams[i], jnp.zeros((1, 128), jnp.float32)
    )
    small[0:1, :] = gamma_new
    small[1:2, :] = gamma_new / gamma_row

    def drain(t, _):
        peer = lax.rem(me + t, n)
        rs_arrival(peer).wait_send()
        ag_copy(my_q, my_g, peer).wait_send()
        gm_copy(me, peer).wait_send()
        return 0

    if paired:
        for zz in range(nz):
            x_copy(zz).wait_send()
            ax_copy(2 * zz + x).wait_send()
        for t in range(1, nz):
            z_copy(z, lax.rem(z + t, nz)).wait_send()

    def cv_drain(t, _):
        cv_copy(rank, lax.rem(rank + t, total)).wait_send()
        return 0

    lax.fori_loop(1, n, drain, 0)
    lax.fori_loop(1, total, cv_drain, 0)


def finish(model, resid, direc, grad, small, model_out, resid_out, direc_out, gamma_out, fresh, sem):
    sets = direc.shape[0]
    pieces, _, width = grad.shape
    copies = [
        pltpu.make_async_copy(model, model_out, sem.at[0]),
        pltpu.make_async_copy(resid, resid_out, sem.at[1]),
    ]
    for copy in copies:
        copy.start()
    ratio = to_column(small[1:2, :], sets)
    for p in range(pieces):
        span = slice(p * width, (p + 1) * width)
        fresh[:, span] = grad[p] + ratio * direc[:, span]
    last = pltpu.make_async_copy(fresh, direc_out, sem.at[2])
    last.start()
    gamma_out[...] = small[0, :sets]
    for copy in copies:
        copy.wait()
    last.wait()


def local(n, sensitivity, block_scale, depth_weight, model, residual, direction, gamma):
    rows, cells = sensitivity.shape
    sets = direction.shape[0]
    nr = min(n, rows // BLOCK)
    ns = n // nr
    cr, cs = rows // nr, sets // ns
    paired = ns == 1 and n % 2 == 0 and n > 2 and cs >= 32
    fa, ga = (cs * 3 // 4 // 8 * 8, cs // 2 // 8 * 8) if paired else (0, 0)
    nz, kept = (n // 2, fa) if paired else (1, 8)
    pieces = 4
    f32 = jnp.float32
    hbm = pl.BlockSpec(memory_space=pltpu.HBM)
    vmem = pl.BlockSpec(memory_space=pltpu.VMEM)
    dma = pltpu.SemaphoreType.DMA
    parts = pl.pallas_call(
        functools.partial(kernel, n, nr, ns, fa, ga),
        out_shape=(
            pltpu.VMEM(model.shape, f32),
            pltpu.VMEM(residual.shape, f32),
            pltpu.VMEM(direction.shape, f32),
            pltpu.VMEM((pieces, sets, cells // pieces), f32),
            pltpu.VMEM((8, 128), f32),
        ),
        in_specs=[hbm] * 7,
        out_specs=(vmem,) * 5,
        scratch_shapes=[
            pltpu.SMEM(block_scale.shape[::-1], f32),
            pltpu.VMEM(depth_weight.shape, f32),
            pltpu.VMEM(gamma.shape, f32),
            pltpu.VMEM((nr, cr, cells), jnp.bfloat16),
            pltpu.VMEM((sets, cells), jnp.bfloat16),
            pltpu.VMEM((nr, sets, cr), f32),
            pltpu.VMEM((n, cs - fa, cr), f32),
            pltpu.VMEM((nz, kept, cr), f32),
            pltpu.VMEM((nz, kept, cr), f32),
            pltpu.VMEM((nr, sets, cr), f32),
            pltpu.VMEM((2 * n, 1, 128), f32),
            pltpu.VMEM((pieces, sets, cells // pieces), f32),
            pltpu.VMEM((n, 1, 128), f32),
            dma((nr,)), dma((6,)),
            dma((nz,)), dma((nz,)), dma((nz,)), dma((nz,)),
            dma((nz,)), dma((nz,)), dma((nz,)), dma((nz,)),
            dma((n,)), dma((n,)), dma((n,)), dma((n,)),
            dma((2 * n,)), dma((2 * n,)), dma((pieces,)), dma((pieces,)),
            dma((n,)), dma((n,)),
        ],
        compiler_params=pltpu.CompilerParams(
            collective_id=0, has_side_effects=True, vmem_limit_bytes=56 * 1024 * 1024
        ),
        cost_estimate=pl.CostEstimate(
            flops=4 * rows * cells * sets, bytes_accessed=2 * rows * cells, transcendentals=0
        ),
        name="cgls_iteration",
    )(sensitivity, block_scale.T, depth_weight, model, residual, direction, gamma)
    return pl.pallas_call(
        finish,
        out_shape=(
            jax.ShapeDtypeStruct(model.shape, f32),
            jax.ShapeDtypeStruct(residual.shape, f32),
            jax.ShapeDtypeStruct(direction.shape, f32),
            jax.ShapeDtypeStruct(gamma.shape, f32),
        ),
        in_specs=[vmem] * 5,
        out_specs=(hbm, hbm, hbm, vmem),
        scratch_shapes=[pltpu.VMEM(direction.shape, f32), dma((3,))],
        compiler_params=pltpu.CompilerParams(vmem_limit_bytes=16 * 1024 * 1024),
        name="cgls_results",
    )(*parts)


def solution(mesh):
    in_specs = (
        P(("groups", "dp"), "cell"),
        P(("groups", "dp"), "cell"),
        P(("groups", "cell")),
        P("groups", "cell"),
        P("groups", "dp"),
        P("groups", "cell"),
        P("groups"),
    )
    out_specs = (P("groups", "cell"), P("groups", "dp"), P("groups", "cell"), P("groups"))
    return jax.shard_map(
        functools.partial(local, mesh.shape["cell"]),
        mesh=mesh, in_specs=in_specs, out_specs=out_specs, check_vma=False,
    )
```

```python
import functools

import jax
import jax.numpy as jnp
from jax import lax
from jax.experimental import pallas as pl
from jax.experimental.pallas import tpu as pltpu
from jax.sharding import PartitionSpec as P

EPSILON = 1e-06
BLOCK = 128
MESH = pl.DeviceIdType.MESH


def to_row(column, first):
    shape = (column.shape[0], 128)
    place = lax.broadcasted_iota(jnp.int32, shape, 0) + first
    lane = lax.broadcasted_iota(jnp.int32, shape, 1)
    return jnp.sum(jnp.where(place == lane, column, 0.0), axis=0, keepdims=True)


def to_column(row, count):
    shape = (count, 128)
    place = lax.broadcasted_iota(jnp.int32, shape, 0)
    lane = lax.broadcasted_iota(jnp.int32, shape, 1)
    return jnp.sum(jnp.where(place == lane, row, 0.0), axis=1, keepdims=True)


def kernel(
    n, nr, ns, fa, ga,
    sens_hbm, scale_hbm, depth_hbm, model_hbm, resid_hbm, direc_hbm, gamma_hbm,
    model, resid, direc, grad, small,
    scale, depth, gamma, sens, scaled, part, recv, xin, zin, pred, curv, other, gams,
    sens_sem, load_sem, x_send, x_recv, z_send, z_recv, ax_send, ax_recv, az_send, az_recv,
    rs_send, rs_recv, ag_send, ag_recv, cv_send, cv_recv, dp_send, dp_recv, gm_send, gm_recv,
):
    sets, cells = direc.shape
    cs, cr = sets // ns, recv.shape[2]
    paired = fa > 0
    nz = n // 2
    row_blocks = cr // BLOCK
    col_blocks = cells // BLOCK
    pieces = grad.shape[0]
    width = grad.shape[2]
    total = 2 * n
    me = lax.axis_index("cell")
    core = lax.axis_index("dp")
    rank = me * 2 + core
    my_q = me // ns
    my_g = me % ns
    x = lax.rem(me, 2)
    z = me // 2
    beside = 2 * z + 1 - x

    def chunk_at(t):
        if not paired:
            return lax.rem(my_q + 1 + t, nr)
        return 2 * lax.rem(z + 1 + t, nz) + lax.rem(x + 1 + t // nz, 2)

    def sens_copy(t):
        q = chunk_at(t)
        return pltpu.make_async_copy(
            sens_hbm.at[pl.ds(pl.multiple_of(q * cr, cr), cr), :], sens.at[t], sens_sem.at[t]
        )

    direc_load = pltpu.make_async_copy(direc_hbm, direc, load_sem.at[0])
    direc_load.start()
    depth_load = pltpu.make_async_copy(depth_hbm, depth, load_sem.at[3])
    depth_load.start()
    scale_load = pltpu.make_async_copy(scale_hbm, scale, load_sem.at[4])
    scale_load.start()
    gamma_load = pltpu.make_async_copy(gamma_hbm, gamma, load_sem.at[5])
    gamma_load.start()
    for t in range(nr):
        sens_copy(t).start()
    resid_load = pltpu.make_async_copy(resid_hbm, resid, load_sem.at[1])
    resid_load.start()
    model_load = pltpu.make_async_copy(model_hbm, model, load_sem.at[2])
    model_load.start()

    barrier = pltpu.get_barrier_semaphore()

    def greet(t, _):
        peer = lax.rem(rank + t, total)
        pl.semaphore_signal(
            barrier, inc=1, device_id={"cell": peer // 2, "dp": lax.rem(peer, 2)}, device_id_type=MESH
        )
        return 0

    lax.fori_loop(1, total, greet, 0, unroll=n <= 8)

    depth_load.wait()
    gamma_load.wait()
    scale_load.wait()
    inverse = 1.0 / depth[...].reshape(1, cells)
    gamma_row = jnp.concatenate(
        [gamma[...].reshape(1, sets), jnp.ones((1, 128 - sets), jnp.float32)], axis=1
    )
    direc_load.wait()
    scaled[...] = (direc[...] * inverse).astype(jnp.bfloat16)

    def rs_copy(q, g):
        j = q * ns + g
        return pltpu.make_async_remote_copy(
            src_ref=part.at[q, pl.ds(pl.multiple_of(g * cs + fa, 8), cs - fa), :],
            dst_ref=recv.at[me],
            send_sem=rs_send.at[j],
            recv_sem=rs_recv.at[me],
            device_id={"cell": j},
            device_id_type=MESH,
        )

    def forward(t):
        q = chunk_at(t)
        sens_copy(t).wait()
        accs = [None] * row_blocks
        for b in range(col_blocks):
            tile = lax.dot_general(
                scaled[:, b * BLOCK:(b + 1) * BLOCK],
                sens[t, :, b * BLOCK:(b + 1) * BLOCK],
                (((1,), (1,)), ((), ())),
                preferred_element_type=jnp.float32,
            )
            for a in range(row_blocks):
                term = tile[:, a * BLOCK:(a + 1) * BLOCK] * scale[b, q * row_blocks + a]
                accs[a] = term if accs[a] is None else accs[a] + term
        for a in range(row_blocks):
            part[q, :, a * BLOCK:(a + 1) * BLOCK] = accs[a]
        return q

    def x_copy(zz):
        return pltpu.make_async_remote_copy(
            src_ref=part.at[2 * zz + 1 - x, pl.ds(0, fa), :], dst_ref=xin.at[zz],
            send_sem=x_send.at[zz], recv_sem=x_recv.at[zz],
            device_id={"cell": beside}, device_id_type=MESH,
        )

    def z_copy(slot, zz):
        return pltpu.make_async_remote_copy(
            src_ref=part.at[2 * zz + x, pl.ds(0, fa), :], dst_ref=zin.at[slot],
            send_sem=z_send.at[zz], recv_sem=z_recv.at[slot],
            device_id={"cell": 2 * zz + x}, device_id_type=MESH,
        )

    if paired:
        def across(t, _):
            q = forward(t)

            @pl.when(t == 0)
            def _():
                pl.semaphore_wait(barrier, total - 1)

            x_copy(q // 2).start()
            rs_copy(q, 0).start()
            return 0

        def along(t, _):
            rs_copy(forward(t), 0).start()
            return 0

        def pass_on(t, _):
            zz = lax.rem(z + 1 + t, nz)
            x_copy(zz).wait_recv()
            part[2 * zz + x, :fa, :] += xin[zz]
            z_copy(z, zz).start()
            return 0

        lax.fori_loop(0, nz, across, 0)
        lax.fori_loop(nz, n - 1, along, 0)
        forward(n - 1)
        lax.fori_loop(0, nz - 1, pass_on, 0, unroll=n <= 8)
    else:
        pl.semaphore_wait(barrier, total - 1)

        def spread(t, _):
            q = forward(t)

            def send(g, _):
                @pl.when(q * ns + g != me)
                def _():
                    rs_copy(q, g).start()
                return 0

            lax.fori_loop(0, ns, send, 0)
            return 0

        lax.fori_loop(0, nr, spread, 0)

    mine = pl.ds(pl.multiple_of(my_g * cs, 8), cs)
    direct = pl.ds(pl.multiple_of(my_g * cs + fa, 8), cs - fa)

    def rs_arrival(src):
        return pltpu.make_async_remote_copy(
            src_ref=recv.at[src], dst_ref=recv.at[src], send_sem=rs_send.at[src],
            recv_sem=rs_recv.at[src], device_id={"cell": src}, device_id_type=MESH,
        )

    relayed = (pl.ds(0, max(ga, 8)), pl.ds(fa, cs - fa))
    top = fa if paired else cs

    def ag_copy(q, g, peer):
        ref = pred.at[q, pl.ds(pl.multiple_of(g * cs + ga, 8), top - ga), :]
        return pltpu.make_async_remote_copy(
            src_ref=ref, dst_ref=ref, send_sem=ag_send.at[peer],
            recv_sem=ag_recv.at[q * ns + g], device_id={"cell": peer}, device_id_type=MESH,
        )

    def az_copy(k, owner, zz):
        ref = pred.at[owner, relayed[k], :]
        return pltpu.make_async_remote_copy(
            src_ref=ref, dst_ref=ref, send_sem=az_send.at[k, zz], recv_sem=az_recv.at[k, owner // 2],
            device_id={"cell": 2 * zz + x}, device_id_type=MESH,
        )

    def ax_copy(k, owner):
        ref = pred.at[owner, relayed[k], :]
        return pltpu.make_async_remote_copy(
            src_ref=ref, dst_ref=ref, send_sem=ax_send.at[k, owner // 2],
            recv_sem=ax_recv.at[k, owner // 2], device_id={"cell": beside}, device_id_type=MESH,
        )

    def relay_start(k):
        for t in range(1, nz):
            az_copy(k, me, lax.rem(z + t, nz)).start()
        ax_copy(k, me).start()

    def relay(k):
        for t in range(1, nz):
            zz = lax.rem(z + nz - t, nz)
            az_copy(k, 2 * zz + x, zz).wait_recv()
            ax_copy(k, 2 * zz + x).start()

    pred[my_q, mine, :] = part[my_q, mine, :]

    def reduce(t, _):
        src = lax.rem(me + t, n)
        rs_arrival(src).wait_recv()
        pred[my_q, direct, :] += recv[src]
        return 0

    lax.fori_loop(1, n, reduce, 0, unroll=n <= 8)

    if paired:
        relay_start(1)
        x_copy(z).wait_recv()
        pred[me, :fa, :] += xin[z]

        def reduce_z(t, _):
            zz = lax.rem(z + t, nz)
            z_copy(zz, zz).wait_recv()
            pred[me, :fa, :] += zin[zz]
            return 0

        lax.fori_loop(1, nz, reduce_z, 0, unroll=n <= 8)

    if paired:
        relay_start(0)
        relay(1)

    value = pred[my_q, mine, :]
    curv[rank] = to_row(jnp.sum(value * value, axis=1, keepdims=True), my_g * cs)

    def cv_copy(slot, peer):
        return pltpu.make_async_remote_copy(
            src_ref=curv.at[slot], dst_ref=curv.at[slot], send_sem=cv_send.at[peer],
            recv_sem=cv_recv.at[slot],
            device_id={"cell": peer // 2, "dp": lax.rem(peer, 2)}, device_id_type=MESH,
        )

    def cv_start(t, _):
        cv_copy(rank, lax.rem(rank + t, total)).start()
        return 0

    lax.fori_loop(1, total, cv_start, 0, unroll=n <= 8)

    if paired:
        for t in range(1, nz):
            az_copy(0, me, lax.rem(z + t, nz)).wait_send()
        for t in range(1, nz):
            ag_copy(me, 0, 2 * lax.rem(z + t, nz) + x).start()
        for t in range(nz):
            ag_copy(me, 0, 2 * lax.rem(z + t, nz) + 1 - x).start()
        relay(0)
    else:
        def ag_start(t, _):
            ag_copy(my_q, my_g, lax.rem(me + t, n)).start()
            return 0

        lax.fori_loop(1, n, ag_start, 0)

    def cv_wait(t, _):
        peer = lax.rem(rank + t, total)
        cv_copy(peer, peer).wait_recv()
        return 0

    lax.fori_loop(1, total, cv_wait, 0, unroll=n <= 8)
    curvature = lax.fori_loop(
        0, total, lambda i, acc: acc + curv[i], jnp.zeros((1, 128), jnp.float32), unroll=n <= 8
    )
    step = to_column(gamma_row / (curvature + EPSILON), sets)

    model_load.wait()
    model[...] = model[...] + step * direc[...]
    resid_load.wait()
    grad[...] = jnp.zeros(grad.shape, jnp.float32)

    def dp_copy(p):
        return pltpu.make_async_remote_copy(
            src_ref=grad.at[p], dst_ref=other.at[p], send_sem=dp_send.at[p],
            recv_sem=dp_recv.at[p], device_id={"dp": 1 - core}, device_id_type=MESH,
        )

    def backward(t, last):
        q = chunk_at(t)

        def arrive(g, _):
            @pl.when(q * ns + g != me)
            def _():
                ag_copy(q, g, q * ns + g).wait_recv()
            return 0

        if not last or not paired:
            lax.fori_loop(0, ns, arrive, 0)
        else:
            ag_copy(q, 0, q).wait_recv()
        where = pl.ds(pl.multiple_of(q * cr, cr), cr)
        fresh = resid[:, where] - step * pred[q]
        resid[:, where] = fresh
        weighted = fresh.astype(jnp.bfloat16)
        for p in range(pieces):
            acc = grad[p]
            for a in range(row_blocks):
                tile = jnp.dot(
                    weighted[:, a * BLOCK:(a + 1) * BLOCK],
                    sens[t, a * BLOCK:(a + 1) * BLOCK, p * width:(p + 1) * width],
                    preferred_element_type=jnp.float32,
                )
                acc = acc + jnp.concatenate(
                    [
                        tile[:, b * BLOCK:(b + 1) * BLOCK]
                        * scale[p * (width // BLOCK) + b, q * row_blocks + a]
                        for b in range(width // BLOCK)
                    ],
                    axis=1,
                )
            grad[p] = acc
            if last:
                dp_copy(p).start()

    def own_column(u, _):
        backward(nr - 1 - u, False)
        return 0

    def other_column(u, _):
        t = nr - 1 - u
        for k in range(2):
            ax_copy(k, 2 * (chunk_at(t) // 2) + x).wait_recv()
        backward(t, False)
        return 0

    if paired:
        lax.fori_loop(0, nz, own_column, 0)
        lax.fori_loop(nz, nr - 1, other_column, 0)
        for k in range(2):
            ax_copy(k, 2 * (chunk_at(0) // 2) + x).wait_recv()
    else:
        lax.fori_loop(0, nr - 1, own_column, 0)
    backward(0, True)

    square = jnp.zeros((sets, 1), jnp.float32)
    for p in range(pieces):
        dp_copy(p).wait()
        full = (grad[p] + other[p]) * inverse[:, p * width:(p + 1) * width]
        grad[p] = full
        square = square + jnp.sum(full * full, axis=1, keepdims=True)
    gams[me] = to_row(square, 0)

    def gm_copy(slot, peer):
        return pltpu.make_async_remote_copy(
            src_ref=gams.at[slot], dst_ref=gams.at[slot], send_sem=gm_send.at[peer],
            recv_sem=gm_recv.at[slot], device_id={"cell": peer}, device_id_type=MESH,
        )

    def gm_start(t, _):
        gm_copy(me, lax.rem(me + t, n)).start()
        return 0

    def gm_wait(t, _):
        peer = lax.rem(me + t, n)
        gm_copy(peer, peer).wait_recv()
        return 0

    lax.fori_loop(1, n, gm_start, 0, unroll=n <= 8)
    lax.fori_loop(1, n, gm_wait, 0, unroll=n <= 8)
    gamma_new = lax.fori_loop(
        0, n, lambda i, acc: acc + gams[i], jnp.zeros((1, 128), jnp.float32), unroll=n <= 8
    )
    small[0:1, :] = gamma_new
    small[1:2, :] = gamma_new / gamma_row

    def drain(t, _):
        peer = lax.rem(me + t, n)
        rs_arrival(peer).wait_send()
        ag_copy(my_q, my_g, peer).wait_send()
        gm_copy(me, peer).wait_send()
        return 0

    if paired:
        for zz in range(nz):
            x_copy(zz).wait_send()
            for k in range(2):
                ax_copy(k, 2 * zz + x).wait_send()
        for t in range(1, nz):
            z_copy(z, lax.rem(z + t, nz)).wait_send()
            az_copy(1, me, lax.rem(z + t, nz)).wait_send()

    def cv_drain(t, _):
        cv_copy(rank, lax.rem(rank + t, total)).wait_send()
        return 0

    lax.fori_loop(1, n, drain, 0, unroll=n <= 8)
    lax.fori_loop(1, total, cv_drain, 0, unroll=n <= 8)


def finish(model, resid, direc, grad, small, model_out, resid_out, direc_out, gamma_out, fresh, sem):
    sets = direc.shape[0]
    pieces, _, width = grad.shape
    copies = [
        pltpu.make_async_copy(model, model_out, sem.at[0]),
        pltpu.make_async_copy(resid, resid_out, sem.at[1]),
    ]
    for copy in copies:
        copy.start()
    ratio = to_column(small[1:2, :], sets)
    for p in range(pieces):
        span = slice(p * width, (p + 1) * width)
        fresh[:, span] = grad[p] + ratio * direc[:, span]
    last = pltpu.make_async_copy(fresh, direc_out, sem.at[2])
    last.start()
    gamma_out[...] = small[0, :sets]
    for copy in copies:
        copy.wait()
    last.wait()


def local(n, sensitivity, block_scale, depth_weight, model, residual, direction, gamma):
    rows, cells = sensitivity.shape
    sets = direction.shape[0]
    nr = min(n, rows // BLOCK)
    ns = n // nr
    cr, cs = rows // nr, sets // ns
    paired = ns == 1 and n % 2 == 0 and n > 2 and cs >= 32
    fa, ga = (cs * 5 // 8 // 8 * 8, cs * 3 // 8 // 8 * 8) if paired else (0, 0)
    nz, kept = (n // 2, fa) if paired else (1, 8)
    pieces = 4
    f32 = jnp.float32
    hbm = pl.BlockSpec(memory_space=pltpu.HBM)
    vmem = pl.BlockSpec(memory_space=pltpu.VMEM)
    dma = pltpu.SemaphoreType.DMA
    parts = pl.pallas_call(
        functools.partial(kernel, n, nr, ns, fa, ga),
        out_shape=(
            pltpu.VMEM(model.shape, f32),
            pltpu.VMEM(residual.shape, f32),
            pltpu.VMEM(direction.shape, f32),
            pltpu.VMEM((pieces, sets, cells // pieces), f32),
            pltpu.VMEM((8, 128), f32),
        ),
        in_specs=[hbm] * 7,
        out_specs=(vmem,) * 5,
        scratch_shapes=[
            pltpu.SMEM(block_scale.shape[::-1], f32),
            pltpu.VMEM(depth_weight.shape, f32),
            pltpu.VMEM(gamma.shape, f32),
            pltpu.VMEM((nr, cr, cells), jnp.bfloat16),
            pltpu.VMEM((sets, cells), jnp.bfloat16),
            pltpu.VMEM((nr, sets, cr), f32),
            pltpu.VMEM((n, cs - fa, cr), f32),
            pltpu.VMEM((nz, kept, cr), f32),
            pltpu.VMEM((nz, kept, cr), f32),
            pltpu.VMEM((nr, sets, cr), f32),
            pltpu.VMEM((2 * n, 1, 128), f32),
            pltpu.VMEM((pieces, sets, cells // pieces), f32),
            pltpu.VMEM((n, 1, 128), f32),
            dma((nr,)), dma((6,)),
            dma((nz,)), dma((nz,)), dma((nz,)), dma((nz,)),
            dma((2, nz)), dma((2, nz)), dma((2, nz)), dma((2, nz)),
            dma((n,)), dma((n,)), dma((n,)), dma((n,)),
            dma((2 * n,)), dma((2 * n,)), dma((pieces,)), dma((pieces,)),
            dma((n,)), dma((n,)),
        ],
        compiler_params=pltpu.CompilerParams(
            collective_id=0, has_side_effects=True, vmem_limit_bytes=56 * 1024 * 1024
        ),
        cost_estimate=pl.CostEstimate(
            flops=4 * rows * cells * sets, bytes_accessed=2 * rows * cells, transcendentals=0
        ),
        name="cgls_iteration",
    )(sensitivity, block_scale.T, depth_weight, model, residual, direction, gamma)
    return pl.pallas_call(
        finish,
        out_shape=(
            jax.ShapeDtypeStruct(model.shape, f32),
            jax.ShapeDtypeStruct(residual.shape, f32),
            jax.ShapeDtypeStruct(direction.shape, f32),
            jax.ShapeDtypeStruct(gamma.shape, f32),
        ),
        in_specs=[vmem] * 5,
        out_specs=(hbm, hbm, hbm, vmem),
        scratch_shapes=[pltpu.VMEM(direction.shape, f32), dma((3,))],
        compiler_params=pltpu.CompilerParams(vmem_limit_bytes=16 * 1024 * 1024),
        name="cgls_results",
    )(*parts)


def solution(mesh):
    in_specs = (
        P(("groups", "dp"), "cell"),
        P(("groups", "dp"), "cell"),
        P(("groups", "cell")),
        P("groups", "cell"),
        P("groups", "dp"),
        P("groups", "cell"),
        P("groups"),
    )
    out_specs = (P("groups", "cell"), P("groups", "dp"), P("groups", "cell"), P("groups"))
    return jax.shard_map(
        functools.partial(local, mesh.shape["cell"]),
        mesh=mesh, in_specs=in_specs, out_specs=out_specs, check_vma=False,
    )
```

```python
import functools

import jax
import jax.numpy as jnp
from jax import lax
from jax.experimental import pallas as pl
from jax.experimental.pallas import tpu as pltpu
from jax.sharding import PartitionSpec as P

EPSILON = 1e-06
BLOCK = 128
MESH = pl.DeviceIdType.MESH


def to_row(column, first):
    shape = (column.shape[0], 128)
    place = lax.broadcasted_iota(jnp.int32, shape, 0) + first
    lane = lax.broadcasted_iota(jnp.int32, shape, 1)
    return jnp.sum(jnp.where(place == lane, column, 0.0), axis=0, keepdims=True)


def to_column(row, count):
    shape = (count, 128)
    place = lax.broadcasted_iota(jnp.int32, shape, 0)
    lane = lax.broadcasted_iota(jnp.int32, shape, 1)
    return jnp.sum(jnp.where(place == lane, row, 0.0), axis=1, keepdims=True)


def kernel(
    n, nr, ns, fa, ga,
    sens_hbm, scale_hbm, depth_hbm, model_hbm, resid_hbm, direc_hbm, gamma_hbm,
    model, resid, direc, grad, small,
    scale, depth, gamma, sens, scaled, part, recv, xin, zin, pred, curv, other, gams,
    sens_sem, load_sem, x_send, x_recv, z_send, z_recv, ax_send, ax_recv, az_send, az_recv,
    rs_send, rs_recv, ag_send, ag_recv, cv_send, cv_recv, dp_send, dp_recv, gm_send, gm_recv,
):
    sets, cells = direc.shape
    cs, cr = sets // ns, recv.shape[2]
    paired = fa > 0
    nz = n // 2
    row_blocks = cr // BLOCK
    col_blocks = cells // BLOCK
    pieces = grad.shape[0]
    width = grad.shape[2]
    total = 2 * n
    me = lax.axis_index("cell")
    core = lax.axis_index("dp")
    rank = me * 2 + core
    my_q = me // ns
    my_g = me % ns
    x = lax.rem(me, 2)
    z = me // 2
    beside = 2 * z + 1 - x

    def chunk_at(t):
        if not paired:
            return lax.rem(my_q + 1 + t, nr)
        return 2 * lax.rem(z + 1 + t, nz) + lax.rem(x + 1 + t // nz, 2)

    def sens_copy(t):
        q = chunk_at(t)
        return pltpu.make_async_copy(
            sens_hbm.at[pl.ds(pl.multiple_of(q * cr, cr), cr), :], sens.at[t], sens_sem.at[t]
        )

    direc_load = pltpu.make_async_copy(direc_hbm, direc, load_sem.at[0])
    direc_load.start()
    depth_load = pltpu.make_async_copy(depth_hbm, depth, load_sem.at[3])
    depth_load.start()
    scale_load = pltpu.make_async_copy(scale_hbm, scale, load_sem.at[4])
    scale_load.start()
    gamma_load = pltpu.make_async_copy(gamma_hbm, gamma, load_sem.at[5])
    gamma_load.start()
    for t in range(nr):
        sens_copy(t).start()
    resid_load = pltpu.make_async_copy(resid_hbm, resid, load_sem.at[1])
    resid_load.start()
    model_load = pltpu.make_async_copy(model_hbm, model, load_sem.at[2])
    model_load.start()

    barrier = pltpu.get_barrier_semaphore()

    def greet(t, _):
        peer = lax.rem(rank + t, total)
        pl.semaphore_signal(
            barrier, inc=1, device_id={"cell": peer // 2, "dp": lax.rem(peer, 2)}, device_id_type=MESH
        )
        return 0

    lax.fori_loop(1, total, greet, 0, unroll=n <= 8)

    depth_load.wait()
    gamma_load.wait()
    scale_load.wait()
    inverse = 1.0 / depth[...].reshape(1, cells)
    gamma_row = jnp.concatenate(
        [gamma[...].reshape(1, sets), jnp.ones((1, 128 - sets), jnp.float32)], axis=1
    )
    direc_load.wait()
    scaled[...] = (direc[...] * inverse).astype(jnp.bfloat16)

    def rs_copy(q, g):
        j = q * ns + g
        return pltpu.make_async_remote_copy(
            src_ref=part.at[q, pl.ds(pl.multiple_of(g * cs + fa, 8), cs - fa), :],
            dst_ref=recv.at[me],
            send_sem=rs_send.at[j],
            recv_sem=rs_recv.at[me],
            device_id={"cell": j},
            device_id_type=MESH,
        )

    def forward(t):
        q = chunk_at(t)
        sens_copy(t).wait()
        accs = [None] * row_blocks
        for b in range(col_blocks):
            tile = lax.dot_general(
                scaled[:, b * BLOCK:(b + 1) * BLOCK],
                sens[t, :, b * BLOCK:(b + 1) * BLOCK],
                (((1,), (1,)), ((), ())),
                preferred_element_type=jnp.float32,
            )
            for a in range(row_blocks):
                term = tile[:, a * BLOCK:(a + 1) * BLOCK] * scale[b, q * row_blocks + a]
                accs[a] = term if accs[a] is None else accs[a] + term
        for a in range(row_blocks):
            part[q, :, a * BLOCK:(a + 1) * BLOCK] = accs[a]
        return q

    def x_copy(zz):
        return pltpu.make_async_remote_copy(
            src_ref=part.at[2 * zz + 1 - x, pl.ds(0, fa), :], dst_ref=xin.at[zz],
            send_sem=x_send.at[zz], recv_sem=x_recv.at[zz],
            device_id={"cell": beside}, device_id_type=MESH,
        )

    def z_copy(slot, zz):
        return pltpu.make_async_remote_copy(
            src_ref=part.at[2 * zz + x, pl.ds(0, fa), :], dst_ref=zin.at[slot],
            send_sem=z_send.at[zz], recv_sem=z_recv.at[slot],
            device_id={"cell": 2 * zz + x}, device_id_type=MESH,
        )

    if paired:
        def across(t, _):
            q = forward(t)

            @pl.when(t == 0)
            def _():
                pl.semaphore_wait(barrier, total - 1)

            x_copy(q // 2).start()
            rs_copy(q, 0).start()
            return 0

        def along(t, _):
            rs_copy(forward(t), 0).start()
            return 0

        def pass_on(t, _):
            zz = lax.rem(z + 1 + t, nz)
            x_copy(zz).wait_recv()
            part[2 * zz + x, :fa, :] += xin[zz]
            z_copy(z, zz).start()
            return 0

        lax.fori_loop(0, nz, across, 0)
        lax.fori_loop(nz, n - 1, along, 0)
        lax.fori_loop(0, nz - 1, pass_on, 0, unroll=n <= 8)
        forward(n - 1)
    else:
        pl.semaphore_wait(barrier, total - 1)

        def spread(t, _):
            q = forward(t)

            def send(g, _):
                @pl.when(q * ns + g != me)
                def _():
                    rs_copy(q, g).start()
                return 0

            lax.fori_loop(0, ns, send, 0)
            return 0

        lax.fori_loop(0, nr, spread, 0)

    mine = pl.ds(pl.multiple_of(my_g * cs, 8), cs)
    direct = pl.ds(pl.multiple_of(my_g * cs + fa, 8), cs - fa)

    def rs_arrival(src):
        return pltpu.make_async_remote_copy(
            src_ref=recv.at[src], dst_ref=recv.at[src], send_sem=rs_send.at[src],
            recv_sem=rs_recv.at[src], device_id={"cell": src}, device_id_type=MESH,
        )

    relayed = (pl.ds(0, max(ga, 8)), pl.ds(fa, cs - fa))
    top = fa if paired else cs

    def ag_copy(q, g, peer):
        ref = pred.at[q, pl.ds(pl.multiple_of(g * cs + ga, 8), top - ga), :]
        return pltpu.make_async_remote_copy(
            src_ref=ref, dst_ref=ref, send_sem=ag_send.at[peer],
            recv_sem=ag_recv.at[q * ns + g], device_id={"cell": peer}, device_id_type=MESH,
        )

    def az_copy(k, owner, zz):
        ref = pred.at[owner, relayed[k], :]
        return pltpu.make_async_remote_copy(
            src_ref=ref, dst_ref=ref, send_sem=az_send.at[k, zz], recv_sem=az_recv.at[k, owner // 2],
            device_id={"cell": 2 * zz + x}, device_id_type=MESH,
        )

    def ax_copy(k, owner):
        ref = pred.at[owner, relayed[k], :]
        return pltpu.make_async_remote_copy(
            src_ref=ref, dst_ref=ref, send_sem=ax_send.at[k, owner // 2],
            recv_sem=ax_recv.at[k, owner // 2], device_id={"cell": beside}, device_id_type=MESH,
        )

    def relay_start(k):
        for t in range(1, nz):
            az_copy(k, me, lax.rem(z + t, nz)).start()
        ax_copy(k, me).start()

    def relay(k):
        for t in range(1, nz):
            zz = lax.rem(z + nz - t, nz)
            az_copy(k, 2 * zz + x, zz).wait_recv()
            ax_copy(k, 2 * zz + x).start()

    pred[my_q, mine, :] = part[my_q, mine, :]

    def reduce(t, _):
        src = lax.rem(me + t, n)
        rs_arrival(src).wait_recv()
        pred[my_q, direct, :] += recv[src]
        return 0

    lax.fori_loop(1, n, reduce, 0, unroll=n <= 8)

    if paired:
        relay_start(1)
        x_copy(z).wait_recv()
        pred[me, :fa, :] += xin[z]

        def reduce_z(t, _):
            zz = lax.rem(z + t, nz)
            z_copy(zz, zz).wait_recv()
            pred[me, :fa, :] += zin[zz]
            return 0

        lax.fori_loop(1, nz, reduce_z, 0, unroll=n <= 8)

    if paired:
        relay_start(0)
        relay(1)

    value = pred[my_q, mine, :]
    curv[rank] = to_row(jnp.sum(value * value, axis=1, keepdims=True), my_g * cs)

    def cv_copy(slot, peer):
        return pltpu.make_async_remote_copy(
            src_ref=curv.at[slot], dst_ref=curv.at[slot], send_sem=cv_send.at[peer],
            recv_sem=cv_recv.at[slot],
            device_id={"cell": peer // 2, "dp": lax.rem(peer, 2)}, device_id_type=MESH,
        )

    def cv_start(t, _):
        cv_copy(rank, lax.rem(rank + t, total)).start()
        return 0

    lax.fori_loop(1, total, cv_start, 0, unroll=n <= 8)

    if paired:
        for t in range(1, nz):
            az_copy(0, me, lax.rem(z + t, nz)).wait_send()
        for t in range(1, nz):
            ag_copy(me, 0, 2 * lax.rem(z + t, nz) + x).start()
        for t in range(nz):
            ag_copy(me, 0, 2 * lax.rem(z + t, nz) + 1 - x).start()
        relay(0)
    else:
        def ag_start(t, _):
            ag_copy(my_q, my_g, lax.rem(me + t, n)).start()
            return 0

        lax.fori_loop(1, n, ag_start, 0)

    def cv_wait(t, _):
        peer = lax.rem(rank + t, total)
        cv_copy(peer, peer).wait_recv()
        return 0

    lax.fori_loop(1, total, cv_wait, 0, unroll=n <= 8)
    curvature = lax.fori_loop(
        0, total, lambda i, acc: acc + curv[i], jnp.zeros((1, 128), jnp.float32), unroll=n <= 8
    )
    step = to_column(gamma_row / (curvature + EPSILON), sets)

    model_load.wait()
    model[...] = model[...] + step * direc[...]
    resid_load.wait()
    grad[...] = jnp.zeros(grad.shape, jnp.float32)

    def dp_copy(p):
        return pltpu.make_async_remote_copy(
            src_ref=grad.at[p], dst_ref=other.at[p], send_sem=dp_send.at[p],
            recv_sem=dp_recv.at[p], device_id={"dp": 1 - core}, device_id_type=MESH,
        )

    def backward(t, last):
        q = chunk_at(t)

        def arrive(g, _):
            @pl.when(q * ns + g != me)
            def _():
                ag_copy(q, g, q * ns + g).wait_recv()
            return 0

        if not last or not paired:
            lax.fori_loop(0, ns, arrive, 0)
        else:
            ag_copy(q, 0, q).wait_recv()
        where = pl.ds(pl.multiple_of(q * cr, cr), cr)
        fresh = resid[:, where] - step * pred[q]
        resid[:, where] = fresh
        weighted = fresh.astype(jnp.bfloat16)
        for p in range(pieces):
            acc = grad[p]
            for a in range(row_blocks):
                tile = jnp.dot(
                    weighted[:, a * BLOCK:(a + 1) * BLOCK],
                    sens[t, a * BLOCK:(a + 1) * BLOCK, p * width:(p + 1) * width],
                    preferred_element_type=jnp.float32,
                )
                acc = acc + jnp.concatenate(
                    [
                        tile[:, b * BLOCK:(b + 1) * BLOCK]
                        * scale[p * (width // BLOCK) + b, q * row_blocks + a]
                        for b in range(width // BLOCK)
                    ],
                    axis=1,
                )
            grad[p] = acc
            if last:
                dp_copy(p).start()

    def own_column(u, _):
        backward(nr - 1 - u, False)
        return 0

    def other_column(u, _):
        t = nr - 1 - u
        for k in range(2):
            ax_copy(k, 2 * (chunk_at(t) // 2) + x).wait_recv()
        backward(t, False)
        return 0

    if paired:
        lax.fori_loop(0, nz, own_column, 0)
        lax.fori_loop(nz, nr - 1, other_column, 0)
        for k in range(2):
            ax_copy(k, 2 * (chunk_at(0) // 2) + x).wait_recv()
    else:
        lax.fori_loop(0, nr - 1, own_column, 0)
    backward(0, True)

    square = jnp.zeros((sets, 1), jnp.float32)
    for p in range(pieces):
        dp_copy(p).wait()
        full = (grad[p] + other[p]) * inverse[:, p * width:(p + 1) * width]
        grad[p] = full
        square = square + jnp.sum(full * full, axis=1, keepdims=True)
    gams[me] = to_row(square, 0)

    def gm_copy(slot, peer):
        return pltpu.make_async_remote_copy(
            src_ref=gams.at[slot], dst_ref=gams.at[slot], send_sem=gm_send.at[peer],
            recv_sem=gm_recv.at[slot], device_id={"cell": peer}, device_id_type=MESH,
        )

    def gm_start(t, _):
        gm_copy(me, lax.rem(me + t, n)).start()
        return 0

    def gm_wait(t, _):
        peer = lax.rem(me + t, n)
        gm_copy(peer, peer).wait_recv()
        return 0

    lax.fori_loop(1, n, gm_start, 0, unroll=n <= 8)
    lax.fori_loop(1, n, gm_wait, 0, unroll=n <= 8)
    gamma_new = lax.fori_loop(
        0, n, lambda i, acc: acc + gams[i], jnp.zeros((1, 128), jnp.float32), unroll=n <= 8
    )
    small[0:1, :] = gamma_new
    small[1:2, :] = gamma_new / gamma_row

    def drain(t, _):
        peer = lax.rem(me + t, n)
        rs_arrival(peer).wait_send()
        ag_copy(my_q, my_g, peer).wait_send()
        gm_copy(me, peer).wait_send()
        return 0

    if paired:
        for zz in range(nz):
            x_copy(zz).wait_send()
            for k in range(2):
                ax_copy(k, 2 * zz + x).wait_send()
        for t in range(1, nz):
            z_copy(z, lax.rem(z + t, nz)).wait_send()
            az_copy(1, me, lax.rem(z + t, nz)).wait_send()

    def cv_drain(t, _):
        cv_copy(rank, lax.rem(rank + t, total)).wait_send()
        return 0

    lax.fori_loop(1, n, drain, 0, unroll=n <= 8)
    lax.fori_loop(1, total, cv_drain, 0, unroll=n <= 8)


def finish(model, resid, direc, grad, small, model_out, resid_out, direc_out, gamma_out, fresh, sem):
    sets = direc.shape[0]
    pieces, _, width = grad.shape
    copies = [
        pltpu.make_async_copy(model, model_out, sem.at[0]),
        pltpu.make_async_copy(resid, resid_out, sem.at[1]),
    ]
    for copy in copies:
        copy.start()
    ratio = to_column(small[1:2, :], sets)
    for p in range(pieces):
        span = slice(p * width, (p + 1) * width)
        fresh[:, span] = grad[p] + ratio * direc[:, span]
        copies.append(pltpu.make_async_copy(fresh.at[:, span], direc_out.at[:, span], sem.at[2 + p]))
        copies[-1].start()
    gamma_out[...] = small[0, :sets]
    for copy in copies:
        copy.wait()


def local(n, sensitivity, block_scale, depth_weight, model, residual, direction, gamma):
    rows, cells = sensitivity.shape
    sets = direction.shape[0]
    nr = min(n, rows // BLOCK)
    ns = n // nr
    cr, cs = rows // nr, sets // ns
    paired = ns == 1 and n % 2 == 0 and n > 2 and cs >= 32
    fa, ga = (cs * 5 // 8 // 8 * 8, cs * 3 // 8 // 8 * 8) if paired else (0, 0)
    nz, kept = (n // 2, fa) if paired else (1, 8)
    pieces = 4
    f32 = jnp.float32
    hbm = pl.BlockSpec(memory_space=pltpu.HBM)
    vmem = pl.BlockSpec(memory_space=pltpu.VMEM)
    dma = pltpu.SemaphoreType.DMA
    parts = pl.pallas_call(
        functools.partial(kernel, n, nr, ns, fa, ga),
        out_shape=(
            pltpu.VMEM(model.shape, f32),
            pltpu.VMEM(residual.shape, f32),
            pltpu.VMEM(direction.shape, f32),
            pltpu.VMEM((pieces, sets, cells // pieces), f32),
            pltpu.VMEM((8, 128), f32),
        ),
        in_specs=[hbm] * 7,
        out_specs=(vmem,) * 5,
        scratch_shapes=[
            pltpu.SMEM(block_scale.shape[::-1], f32),
            pltpu.VMEM(depth_weight.shape, f32),
            pltpu.VMEM(gamma.shape, f32),
            pltpu.VMEM((nr, cr, cells), jnp.bfloat16),
            pltpu.VMEM((sets, cells), jnp.bfloat16),
            pltpu.VMEM((nr, sets, cr), f32),
            pltpu.VMEM((n, cs - fa, cr), f32),
            pltpu.VMEM((nz, kept, cr), f32),
            pltpu.VMEM((nz, kept, cr), f32),
            pltpu.VMEM((nr, sets, cr), f32),
            pltpu.VMEM((2 * n, 1, 128), f32),
            pltpu.VMEM((pieces, sets, cells // pieces), f32),
            pltpu.VMEM((n, 1, 128), f32),
            dma((nr,)), dma((6,)),
            dma((nz,)), dma((nz,)), dma((nz,)), dma((nz,)),
            dma((2, nz)), dma((2, nz)), dma((2, nz)), dma((2, nz)),
            dma((n,)), dma((n,)), dma((n,)), dma((n,)),
            dma((2 * n,)), dma((2 * n,)), dma((pieces,)), dma((pieces,)),
            dma((n,)), dma((n,)),
        ],
        compiler_params=pltpu.CompilerParams(
            collective_id=0, has_side_effects=True, vmem_limit_bytes=56 * 1024 * 1024
        ),
        cost_estimate=pl.CostEstimate(
            flops=4 * rows * cells * sets, bytes_accessed=2 * rows * cells, transcendentals=0
        ),
        name="cgls_iteration",
    )(sensitivity, block_scale.T, depth_weight, model, residual, direction, gamma)
    return pl.pallas_call(
        finish,
        out_shape=(
            jax.ShapeDtypeStruct(model.shape, f32),
            jax.ShapeDtypeStruct(residual.shape, f32),
            jax.ShapeDtypeStruct(direction.shape, f32),
            jax.ShapeDtypeStruct(gamma.shape, f32),
        ),
        in_specs=[vmem] * 5,
        out_specs=(hbm, hbm, hbm, vmem),
        scratch_shapes=[pltpu.VMEM(direction.shape, f32), dma((2 + pieces,))],
        compiler_params=pltpu.CompilerParams(vmem_limit_bytes=16 * 1024 * 1024),
        name="cgls_results",
    )(*parts)


def solution(mesh):
    in_specs = (
        P(("groups", "dp"), "cell"),
        P(("groups", "dp"), "cell"),
        P(("groups", "cell")),
        P("groups", "cell"),
        P("groups", "dp"),
        P("groups", "cell"),
        P("groups"),
    )
    out_specs = (P("groups", "cell"), P("groups", "dp"), P("groups", "cell"), P("groups"))
    return jax.shard_map(
        functools.partial(local, mesh.shape["cell"]),
        mesh=mesh, in_specs=in_specs, out_specs=out_specs, check_vma=False,
    )
```
